32 devices in a mesh: groups: 2 (over y), rel: 4 (over z), bin: 2 (over x), rep: 2 (over core).
Axes of the slice: x: 2, y: 2, z: 4, core: 2. Of those that a mesh axis runs over, the one named last changes fastest.
Arguments:
- footprint: bfloat16 [192, 128, 128], P(('groups', 'rel', 'bin', 'rep')), parts along dimension 0, as said below
- block_tile: int32 [192], P(('groups', 'rel', 'bin', 'rep')), parts along dimension 0, may hold values from 0 to 31, as said below
- log_release: float32 [1024, 32], P(('groups', 'rel')), parts along dimension 0, may hold values from -4 to 4
- prior_mean: float32 [1024, 32], P(('groups', 'rel')), parts along dimension 0, may hold values from -4 to 4
- prior_weight: float32 [1024, 32], P(('groups', 'rel')), parts along dimension 0, may hold values from 0.5 to 2
- observed: float32 [256, 32, 128], P(('groups', 'rel', 'bin', 'rep')), parts along dimension 0, may hold values from -6 to 6
- noise_weight: float32 [256, 32, 128], P(('groups', 'rel', 'bin', 'rep')), parts along dimension 0, may hold values from 0.5 to 2
- pixel_mask: int32 [256, 128], P(('groups', 'rel', 'bin', 'rep')), parts along dimension 0, may hold values 0 or 1
Outputs:
- release_new: float32 [1024, 32], P(('groups', 'rel'), ('bin', 'rep')), parts along dimension 0
- residual: float32 [256, 32, 128], P(('groups', 'rel', 'bin', 'rep')), parts along dimension 0
The draws below stay inside these ranges and needn't reach their ends.
There are 2 independent parts, one for each index of `groups`. The reference program is written for one: setup_inputs(seed, part) draws one part's arguments, and reference() takes and returns one part's arrays. A program takes and returns all parts, laid end to end along the dimension named above; each array names one. Nothing has to cross between parts.
Inputs may be any that keep to these rules, and one draw needn't show every extreme that they name: `footprint`: Real-valued sensitivities. `block_tile`: values are indices among the 32 swath tiles of the devices with the same bin and rep indices: owner value // 8 along rel, local tile value % 8. A device's list is grouped by owner in ascending order; at most 2 entries name one owner, and those name different tiles. In every group of devices with equal bin and rep indices, one owner is named 2 times by every device of the group.
All inputs are finite; a program needn't handle non-finite values. No bound on the sum of `pixel_mask` on one device may be relied on, other than what follows from the above.
Results may differ from the reference program's by a relative error of at most 0.002.
Values may be sent and summed in bfloat16 or wider, within the bound.
A program may use at most 64 MiB of HBM per device.

```python
import math
import jax
import jax.numpy as jnp
from jax import lax

BINS = 32
REL_DEV = 128
TILE = 128
CAP = 2
TILE_DEV = 8
OWNERS = 4
PLANES = 4
KB = 6
SLOTS = 8
BLOCKS = 96
TILES = 128
RELEASES = 512


def correlation_tables(key):
    devices = OWNERS * PLANES
    hot_owner = jax.random.randint(jax.random.fold_in(key, 11), (PLANES,), 0, OWNERS)
    device_keys = jax.random.split(jax.random.fold_in(key, 12), devices)
    offsets = jax.random.randint(jax.random.fold_in(key, 13), (devices, OWNERS), 0, TILE_DEV)
    slot_owner = jnp.arange(SLOTS, dtype=jnp.int32) // CAP
    within = jnp.arange(CAP, dtype=jnp.int32)

    def one_device(device_key, device, offset_row):
        plane = device % PLANES
        scores = jax.random.permutation(device_key, SLOTS).astype(jnp.int32)
        scores = jnp.where(slot_owner == hot_owner[plane], -1, scores)
        ranked = jnp.argsort(scores, stable=True)
        taken = jnp.zeros((SLOTS,), jnp.int32).at[ranked[:KB]].set(1)
        counts = taken.reshape(OWNERS, CAP).sum(axis=1)
        local = (offset_row[:, None] + within[None, :]) % TILE_DEV
        return jnp.where(within[None, :] < counts[:, None], local, -1).astype(jnp.int32)
    return jax.vmap(one_device)(device_keys, jnp.arange(devices, dtype=jnp.int32), offsets)


def draw_footprint(key, part):
    sigma = (TILE * KB * PLANES / 4.0) ** (-0.5)
    width = REL_DEV / 8.0
    noise = jnp.clip(jax.random.normal(jax.random.fold_in(key, 21), (BLOCKS, REL_DEV, TILE), jnp.float32), -5.0, 5.0)
    signs = (jax.random.randint(jax.random.fold_in(key, 22), (BLOCKS,), 0, 2) * 2 - 1).astype(jnp.float32)
    pattern = jnp.exp(jax.random.uniform(jax.random.fold_in(key, 23), (BLOCKS, TILE), jnp.float32, -1.1, 1.1)) * signs[:, None]
    centre = jax.random.uniform(jax.random.fold_in(key, 24), (BLOCKS,), jnp.float32, 0.0, REL_DEV * 1.0)
    place = jnp.arange(REL_DEV, dtype=jnp.float32)
    apart = jnp.abs(place[None, :] - centre[:, None])
    apart = jnp.minimum(apart, REL_DEV - apart)
    bump = jnp.exp(-0.5 * (apart / width) ** 2)
    rough = jax.random.uniform(jax.random.fold_in(key, 25), (BLOCKS, REL_DEV), jnp.float32, 0.5, 1.5)
    profile = rough * bump
    values = sigma * (noise + profile[:, :, None] * pattern[:, None, :])
    return values.astype(jnp.bfloat16)


def draw_block_tile(key, part):
    tables = correlation_tables(jax.random.fold_in(key, 5))
    owner_ids = jnp.arange(OWNERS, dtype=jnp.int32)[None, :, None]
    values = jnp.where(tables >= 0, owner_ids * TILE_DEV + tables, -1)
    flat = values.reshape(OWNERS * PLANES, SLOTS)
    order = jnp.argsort((flat < 0).astype(jnp.int32), axis=1, stable=True)[:, :KB]
    picked = jnp.take_along_axis(flat, order, axis=1)
    return picked.reshape(BLOCKS).astype(jnp.int32)


def place_ends(values, own_key, smallest, high):
    longest = values.shape.index(max(values.shape))
    spots = []
    for shift in (0, 1):
        where = [jax.random.randint(jax.random.fold_in(own_key, axis), (), 0, length) for axis, length in enumerate(values.shape)]
        where[longest] = (where[longest] + shift) % values.shape[longest]
        spots.append(tuple(where))
    return values.at[spots[0]].set(smallest).at[spots[1]].set(high)


def block_levels(stream_key, extent, cuts, low, top_value):
    gain, own = 1.0, jax.random.fold_in(stream_key, 6)
    for dim, blocks in cuts:
        heights = jnp.exp(jax.random.uniform(jax.random.fold_in(own, dim), (blocks,), jnp.float32, low / len(cuts), top_value / len(cuts)))
        gain = gain * jnp.repeat(heights, extent[dim] // blocks).reshape([-1 if axis == dim else 1 for axis in range(len(extent))])
    return gain


def bell_draw(own_key, shape, deviation, reach, shards=(), kind=jnp.bfloat16):
    array = jax.random.normal(own_key, shape, jnp.float32) * deviation
    if len(shards) > 0:
        array = block_levels(own_key, shape, shards, -0.22, 0.18) * array
    return jnp.clip(array, min=-reach, max=reach).astype(kind)


def setup_inputs(seed: int = 0, part: int = 0) -> dict:
    splits = jax.random.split(jax.random.key(seed), 9)
    own_keys = jax.random.split(jax.random.fold_in(splits[8], part), 9)
    return {
        "footprint": draw_footprint(jax.random.fold_in(jax.random.fold_in(splits[8], part), 71), part),
        "block_tile": draw_block_tile(jax.random.fold_in(jax.random.fold_in(splits[8], part), 71), part),
        "log_release": bell_draw(own_keys[2], (RELEASES, BINS), 1.0, 4.0, ((0, 4),), jnp.float32),
        "prior_mean": bell_draw(own_keys[3], (RELEASES, BINS), 1.0, 4.0, ((0, 4),), jnp.float32),
        "prior_weight": jnp.clip(jnp.exp(math.log(2.0) - 1.3862944 * jax.random.uniform(own_keys[4], (RELEASES, BINS), jnp.float32) ** block_levels(own_keys[4], (RELEASES, BINS), ((0, 4),), -0.2, 0.2)), 0.5, 2.0),
        "observed": bell_draw(own_keys[5], (TILES, BINS, TILE), 1.0, 6.0, ((0, 16),), jnp.float32),
        "noise_weight": jnp.clip(jnp.exp(math.log(2.0) - 1.3862944 * jax.random.uniform(own_keys[6], (TILES, BINS, TILE), jnp.float32) ** block_levels(own_keys[6], (TILES, BINS, TILE), ((0, 16),), -0.2, 0.2)), 0.5, 2.0),
        "pixel_mask": place_ends((jax.random.randint(own_keys[7], (TILES, TILE), 0, 10) < 7).astype(jnp.int32), jax.random.fold_in(own_keys[7], 1), 0, 1),
    }


def newton_update(gram_sum, gradient, release_part, mean_part, weight_part):
    slopes = jax.nn.sigmoid(release_part).T
    prior_diag = weight_part.T
    matrix = slopes[:, :, None] * gram_sum * slopes[:, None, :]
    matrix = 0.5 * (matrix + jnp.swapaxes(matrix, 1, 2))
    identity = jnp.eye(matrix.shape[1], dtype=jnp.float32)
    matrix = matrix + prior_diag[:, :, None] * identity[None]
    right_side = slopes * gradient - prior_diag * (release_part - mean_part).T
    factor = jnp.linalg.cholesky(matrix)
    partial_sol = jax.scipy.linalg.solve_triangular(factor, right_side[:, :, None], lower=True)
    update_step = jax.scipy.linalg.solve_triangular(factor, partial_sol, lower=True, trans=1)[:, :, 0]
    return release_part + update_step.T

def reference(footprint, block_tile, log_release, prior_mean, prior_weight, observed, noise_weight, pixel_mask):
    per_owner = KB * PLANES
    block_plane = jnp.arange(BLOCKS, dtype=jnp.int32) // KB % PLANES
    tile_of = (block_tile // TILE_DEV * PLANES + block_plane) * TILE_DEV + block_tile % TILE_DEV
    rates = jax.nn.softplus(log_release).astype(jnp.bfloat16)
    prints = footprint.reshape(OWNERS, per_owner, REL_DEV, TILE)
    tile_ids = tile_of.reshape(OWNERS, per_owner).astype(jnp.int32)
    owner_rates = rates.reshape(OWNERS, REL_DEV, BINS)

    def add_owner(running, pieces):
        block_prints, block_tiles, block_rates = pieces
        emission = jnp.einsum('rb,krp->kbp', block_rates.astype(jnp.float32), block_prints.astype(jnp.float32))
        return (running + jax.ops.segment_sum(emission, block_tiles, num_segments=TILES), None)
    predicted, _ = lax.scan(add_owner, jnp.zeros((TILES, BINS, TILE), jnp.float32), (prints, tile_ids, owner_rates))
    weight = pixel_mask[:, None, :].astype(jnp.float32) * noise_weight
    residual = weight * (observed - predicted)
    resid_half = residual.astype(jnp.bfloat16)
    weight_half = weight.astype(jnp.bfloat16)
    group = math.gcd(per_owner, 16)

    def solve_owner(pieces):
        block_prints, block_tiles, release_part, mean_part, weight_part = pieces
        prints_wide = block_prints.astype(jnp.float32)
        resid_rows = resid_half[block_tiles].astype(jnp.float32)
        weight_rows = weight_half[block_tiles]
        gradient = jnp.einsum('kbp,krp->br', resid_rows, prints_wide)

        def add_group(counter, running):
            start = (counter * group).astype(jnp.int32)
            group_prints = lax.dynamic_slice_in_dim(prints_wide, start, group, 0)
            group_weights = lax.dynamic_slice_in_dim(weight_rows, start, group, 0).astype(jnp.float32)
            scaled = (group_prints[:, None, :, :] * group_weights[:, :, None, :]).astype(jnp.bfloat16)
            scaled = lax.optimization_barrier(scaled).astype(jnp.float32)
            return running + jnp.einsum('kbrp,ksp->brs', scaled, group_prints)
        gram_sum = lax.fori_loop(0, per_owner // group, add_group, jnp.zeros((BINS, REL_DEV, REL_DEV), jnp.float32))
        return newton_update(gram_sum, gradient, release_part, mean_part, weight_part)
    release_new = lax.map(solve_owner, (prints, tile_ids, log_release.reshape(OWNERS, REL_DEV, BINS), prior_mean.reshape(OWNERS, REL_DEV, BINS), prior_weight.reshape(OWNERS, REL_DEV, BINS)))
    return (release_new.reshape(RELEASES, BINS), residual)
```

```python
import functools
import math

import jax
import jax.numpy as jnp
from jax import lax
from jax.experimental import pallas as pl
from jax.experimental.pallas import tpu as pltpu
from jax.sharding import PartitionSpec as P

MESH = pl.DeviceIdType.MESH
F32, BF16 = jnp.float32, jnp.bfloat16
HIGHEST = lax.Precision.HIGHEST
NN = (((1,), (0,)), ((), ()))
TN = (((0,), (0,)), ((), ()))
PANEL = 32


def dot(a, b, dims=NN, precision=None):
    return lax.dot_general(a, b, dims, precision=precision, preferred_element_type=F32)


def split(x):
    high = x.astype(BF16)
    rest = x - high.astype(F32)
    middle = rest.astype(BF16)
    return high, middle, (rest - middle.astype(F32)).astype(BF16)


def step_kernel(
    owners, xs, share, cap,
    fp_hbm, bt, lr_hbm, mean_hbm, pw_hbm, obs_hbm, noise_hbm, mask_hbm,
    resid_hbm, updated,
    fp, far, obs, noise, resid, lr, mean, pw, mask,
    idx_send, idx_recv, w_send, w_recv, em_send, em_recv, r_send, r_recv,
    weight, ft, w_out, w_in, r_out, r_in, wrows,
    mat, pan,
    in_s, out_s,
    idx_ss, idx_rs, w_ss, w_rs, em_ss, em_rs, r_ss, r_rs,
    wp_ss, wp_rs, rp_ss, rp_rs, fp_ss, fp_rs,
):
    blocks, releases, pixels = fp.shape
    planes = 2 * xs
    tiles, bins, _ = obs.shape
    half = blocks // 2
    pack = 16 // share
    me, mx, mc = lax.axis_index("rel"), lax.axis_index("bin"), lax.axis_index("rep")

    def rel_id(step):
        return {"rel": lax.rem(me + step, owners)}

    def plane_id(dx, dc):
        return {"bin": lax.rem(mx + dx, xs), "rep": lax.rem(mc + dc, 2)}

    others = [(dx, dc) for dx in range(xs) for dc in range(2) if (dx, dc) != (0, 0)]

    def remote(src, dst, ss, rs, target):
        return pltpu.make_async_remote_copy(
            src_ref=src, dst_ref=dst, send_sem=ss, recv_sem=rs, device_id=target,
            device_id_type=MESH,
        )

    loads = [
        pltpu.make_async_copy(src, dst, in_s.at[n])
        for n, (src, dst) in enumerate((
            (lr_hbm, lr), (fp_hbm, fp), (mask_hbm, mask), (noise_hbm, noise), (obs_hbm, obs),
            (mean_hbm, mean), (pw_hbm, pw),
        ))
    ]
    for copy in loads:
        copy.start()
    barrier = pltpu.get_barrier_semaphore()
    for step in range(1, owners):
        pl.semaphore_signal(barrier, inc=1, device_id=rel_id(step), device_id_type=MESH)
    for dx, dc in others:
        pl.semaphore_signal(barrier, inc=1, device_id=plane_id(dx, dc), device_id_type=MESH)

    sub = lax.broadcasted_iota(jnp.int32, (8, pixels), 0)
    slots = {}
    for step in range(owners):
        first_tile = lax.rem(me + step, owners) * tiles
        start, end = jnp.int32(0), jnp.int32(0)
        for k in range(blocks):
            start += (bt[k] < first_tile).astype(jnp.int32)
            end += (bt[k] < first_tile + tiles).astype(jnp.int32)
        table = jnp.full((8, pixels), -1, jnp.int32)
        for j in range(cap):
            source = jnp.minimum(start + j, blocks - 1)
            used = start + j < end
            tile = jnp.where(used, bt[source] - first_tile, -1)
            slots[step, j] = source, used
            table = jnp.where(sub == j, tile, table)
        if step:
            idx_send[step] = table
        else:
            idx_recv[0] = table

    pl.semaphore_wait(barrier, owners - 1 + len(others))
    idx_copies = [
        remote(idx_send.at[s], idx_recv.at[s], idx_ss.at[s], idx_rs.at[s], rel_id(s))
        for s in range(1, owners)
    ]
    for copy in idx_copies:
        copy.start()
    piece = [pl.ds(h * half, half) for h in range(2)]
    across, over = {}, {}
    for h in range(2):
        for dx in range(1, xs):
            across[dx, h] = remote(
                fp_hbm.at[piece[h]], far.at[2 * dx, piece[h]],
                fp_ss.at[2 * dx, h], fp_rs.at[2 * dx, h], plane_id(dx, 0),
            )
            across[dx, h].start()
        over[0, h] = remote(
            fp_hbm.at[piece[h]], far.at[1, piece[h]], fp_ss.at[1, h], fp_rs.at[1, h],
            plane_id(0, 1),
        )
        over[0, h].start()

    loads[0].wait()
    rates = jnp.log1p(jnp.exp(-jnp.abs(lr[...]))) + jnp.maximum(lr[...], 0.0)
    rates = rates.astype(BF16)
    loads[1].wait()
    em_copies = []
    for step in [*range(1, owners), 0]:
        target = em_send if step else em_recv
        for j in range(cap):
            source, used = slots[step, j]
            emission = dot(rates, fp[source])
            target[step, j] = jnp.where(used, emission, 0.0)
        if step:
            copy = remote(
                em_send.at[step], em_recv.at[step], em_ss.at[step], em_rs.at[step], rel_id(step)
            )
            copy.start()
            em_copies.append(copy)

    loads[2].wait()
    loads[3].wait()
    for t in range(tiles):
        weight[t] = mask[t : t + 1, :].astype(F32) * noise[t]

    def turn(slot):
        blocks_here = far.at[slot] if slot else fp
        for k in range(blocks):
            ft[slot, k * pixels : (k + 1) * pixels, :] = blocks_here[k].T

    turn(0)

    back_ids = [rel_id(owners - s) for s in range(owners)]

    def pick(step, j, array):
        row = idx_recv[step][j : j + 1, :]
        total = jnp.zeros(array.shape[1:], F32)
        for t in range(tiles):
            total = jnp.where(row == t, array[t], total)
        return total.astype(BF16)

    w_copies = []
    for step in [*range(1, owners), 0]:
        if step:
            idx_copies[step - 1].wait_recv()
        target = w_send if step else w_recv
        for j in range(cap):
            target[step, j] = pick(step, j, weight)
        if step:
            copy = remote(
                w_send.at[step], w_recv.at[step], w_ss.at[step], w_rs.at[step], back_ids[step]
            )
            copy.start()
            w_copies.append(copy)
    loads[4].wait()
    for copy in em_copies:
        copy.wait_recv()
    for t in range(tiles):
        total = jnp.zeros((bins, pixels), F32)
        for step in range(owners):
            for j in range(cap):
                row = idx_recv[step][j : j + 1, :]
                total += jnp.where(row == t, em_recv[step, j], 0.0)
        resid[t] = weight[t] * (obs[t] - total)
    resid_out = pltpu.make_async_copy(resid, resid_hbm, out_s)
    resid_out.start()
    r_copies = []
    for step in [*range(1, owners), 0]:
        target = r_send if step else r_recv
        for j in range(cap):
            target[step, j] = pick(step, j, resid)
        if step:
            copy = remote(
                r_send.at[step], r_recv.at[step], r_ss.at[step], r_rs.at[step], back_ids[step]
            )
            copy.start()
            r_copies.append(copy)

    for dx in range(1, xs):
        for h in range(2):
            across[dx, h].wait_recv()
            over[dx, h] = remote(
                far.at[2 * dx, piece[h]], far.at[2 * dx + 1, piece[h]],
                fp_ss.at[2 * dx + 1, h], fp_rs.at[2 * dx + 1, h], plane_id(0, 1),
            )
            over[dx, h].start()

    places = []
    for k in range(blocks):
        owner = bt[k] // tiles
        rank = jnp.int32(0)
        for back in range(1, cap):
            if k - back >= 0:
                rank += (bt[k - back] // tiles == owner).astype(jnp.int32)
        places.append((lax.rem(owner - me + owners, owners), rank))

    def to_plane(array, out, arrived, ss, rs):
        for k in range(0, blocks, pack):
            rows = [array[place].astype(F32) for place in places[k : k + pack]]
            for q in range(planes):
                wanted = [row[q * share : (q + 1) * share] for row in rows]
                wanted = jnp.concatenate(wanted, axis=0).astype(BF16)
                out[q, k * share : (k + pack) * share, :] = wanted
        copies = []
        for dx, dc in others:
            target, slot = plane_id(dx, dc), 2 * dx + dc
            copy = remote(
                out.at[target["bin"] * 2 + target["rep"]], arrived.at[slot],
                ss.at[slot], rs.at[slot], target,
            )
            copy.start()
            copies.append(copy)
        return copies

    here = mx * 2 + mc
    for copy in w_copies:
        copy.wait_recv()
    wp_copies = to_plane(w_recv, w_out, w_in, wp_ss, wp_rs)

    group = math.gcd(blocks, 6)

    def gram(slot, fresh):
        blocks_here = far.at[slot] if slot else fp

        def add(start):
            def pair(i, carry):
                rows = []
                for b in range(2):
                    parts = []
                    for n in range(group):
                        w = wrows[pl.ds((start + n) * share + 2 * i + b, 1), :]
                        parts.append(blocks_here[start + n] * w.astype(BF16))
                    rows.append(jnp.concatenate(parts, axis=1))
                turned = ft[slot, pl.ds(pl.multiple_of(start * pixels, 128), group * pixels), :]
                total = dot(jnp.concatenate(rows, axis=0), turned)
                for b in range(2):
                    part = total[b * releases : (b + 1) * releases]
                    mat[2 * i + b] = part if fresh else mat[2 * i + b] + part
                return carry

            lax.fori_loop(0, share // 2, pair, 0)

        if blocks == group:
            add(0)
        else:
            if fresh:
                mat[...] = jnp.zeros_like(mat)
            fresh = False
            lax.fori_loop(0, blocks // group, lambda g, c: (add(g * group), c)[1], 0)

    wrows[...] = w_out[here].astype(F32)
    gram(0, True)

    for copy in r_copies:
        copy.wait_recv()
    rp_copies = to_plane(r_recv, r_out, r_in, rp_ss, rp_rs)

    for n, (dx, dc) in enumerate(others):
        slot = 2 * dx + dc
        for h in range(2):
            if dc:
                over[dx, h].wait_recv()
        wp_copies[n].wait_recv()
        turn(slot)
        wrows[...] = w_in[slot].astype(F32)
        gram(slot, False)

    loads[5].wait()
    loads[6].wait()
    first = (mx * 2 + mc) * share
    want = lax.broadcasted_iota(jnp.int32, (share, bins), 0) + first
    chosen = (lax.broadcasted_iota(jnp.int32, (share, bins), 1) == want).astype(F32)
    lr_t, mean_t, pw_t = (dot(chosen, ref[...], NN, HIGHEST) for ref in (lr, mean, pw))
    inverse_slope = 1.0 + jnp.exp(-lr_t)
    extra = pw_t * inverse_slope * inverse_slope

    row_id = lax.broadcasted_iota(jnp.int32, (releases, releases), 0)
    col_id = lax.broadcasted_iota(jnp.int32, (releases, releases), 1)
    on = row_id == col_id
    for b in range(share):
        square = mat[b]
        square = 0.5 * (square + square.T)
        mat[b] = jnp.where(on, square + extra[b : b + 1], square)

    invert(share, mat, pan)

    def side(array):
        wide = array.astype(F32)
        parts = [wide[k * share : (k + 1) * share] for k in range(blocks)]
        return jnp.concatenate(parts, axis=1).astype(BF16)

    total = dot(side(r_out[here]), ft[0])
    for n, (dx, dc) in enumerate(others):
        rp_copies[n].wait_recv()
        total += dot(side(r_in[2 * dx + dc]), ft[2 * dx + dc])
    right = total - pw_t * (lr_t - mean_t) * inverse_slope
    wide = jnp.concatenate([*split(right), jnp.zeros_like(right, BF16)], axis=0)
    sub_share = lax.broadcasted_iota(jnp.int32, (share, releases), 0)
    change = jnp.zeros((share, releases), F32)
    for b in range(share):
        high, middle, low = (dot(wide, part) for part in split(mat[b]))
        solved = (
            high[:share] + high[share : 2 * share] + high[2 * share : 3 * share]
            + middle[:share] + middle[share : 2 * share] + low[:share]
        )
        change = jnp.where(sub_share == b, solved, change)
    updated[...] = lr_t + change * inverse_slope

    for copy in [
        *idx_copies, *em_copies, *w_copies, *r_copies, *wp_copies, *rp_copies,
        *across.values(), *over.values(),
    ]:
        copy.wait_send()
    resid_out.wait()


def invert(share, mat, pan):
    releases = mat.shape[1]
    lane = lax.broadcasted_iota(jnp.int32, (share, releases), 1)
    col_id = lax.broadcasted_iota(jnp.int32, (releases, releases), 1)
    panel_lane = lax.broadcasted_iota(jnp.int32, (PANEL, releases), 1)
    for base in range(0, releases, PANEL):
        for b in range(share):
            pan[pl.ds(b, PANEL, stride=share), :] = mat[b, base : base + PANEL, :]
        rows = pan[...].reshape(PANEL, share, releases)
        for k in range(0, PANEL, 2):
            c = base + k
            f0 = jnp.broadcast_to(rows[:, :, c : c + 1], rows.shape)
            f1 = jnp.broadcast_to(rows[:, :, c + 1 : c + 2], rows.shape)
            p, q, r, s = f0[k], f1[k], f0[k + 1], f1[k + 1]
            scale = 1.0 / (p * s - q * r)
            at0, at1 = lane == c, lane == c + 1
            u0 = jnp.where(at0, 1.0, jnp.where(at1, 0.0, rows[k]))
            u1 = jnp.where(at1, 1.0, jnp.where(at0, 0.0, rows[k + 1]))
            n0 = (s * u0 - q * u1) * scale
            n1 = (p * u1 - r * u0) * scale
            pivots = jnp.concatenate([n0[None], n1[None]], axis=0)
            gone = (at0 | at1)[None]

            def reduce(a, z):
                kept = jnp.where(gone, 0.0, rows[a:z])
                return kept - f0[a:z] * n0[None] - f1[a:z] * n1[None]

            pieces = [reduce(0, k)] if k else []
            pieces.append(pivots)
            if k + 2 < PANEL:
                pieces.append(reduce(k + 2, PANEL))
            rows = jnp.concatenate(pieces, axis=0)
        pan[...] = rows.reshape(PANEL * share, releases)
        inside = (col_id >= base) & (col_id < base + PANEL)
        for b in range(share):
            old = mat[b]
            side = old[base : base + PANEL]
            side = jnp.where(panel_lane < base, -side, side)
            new = pan[pl.ds(b, PANEL, stride=share), :]
            sh, sm, sl = split(side)
            nh, nm, nl = split(new)
            left = jnp.concatenate([sh, sh, sm, sh, sl, sm], axis=0)
            right = jnp.concatenate([nh, nm, nh, nl, nh, nm], axis=0)
            moved = jnp.where(inside, 0.0, old) - dot(left, right, TN)
            mat[b] = moved
            mat[b, base : base + PANEL, :] = new


def body(
    footprint, block_tile, log_release, prior_mean, prior_weight, observed, noise_weight, pixel_mask
):
    blocks, releases, pixels = footprint.shape
    tiles, bins, _ = observed.shape
    owners, xs = lax.axis_size("rel"), lax.axis_size("bin")
    cap = blocks * 4 // 3 // owners
    planes = 2 * xs
    share = bins // planes
    vmem = pl.BlockSpec(memory_space=pltpu.VMEM)
    smem = pl.BlockSpec(memory_space=pltpu.SMEM)
    dma = pltpu.SemaphoreType.DMA
    slot = (owners, cap, bins, pixels)
    rows = (planes, blocks * share, pixels)
    hbm = pl.BlockSpec(memory_space=pltpu.HBM)
    residual, updated = pl.pallas_call(
        functools.partial(step_kernel, owners, xs, share, cap),
        out_shape=(
            jax.ShapeDtypeStruct(observed.shape, F32),
            jax.ShapeDtypeStruct((share, releases), F32),
        ),
        in_specs=[hbm, smem, hbm, hbm, hbm, hbm, hbm, hbm],
        out_specs=(hbm, vmem),
        scratch_shapes=[
            pltpu.VMEM(footprint.shape, BF16),
            pltpu.VMEM((planes, *footprint.shape), BF16),
            *[pltpu.VMEM(observed.shape, F32) for _ in range(3)],
            *[pltpu.VMEM((bins, releases), F32) for _ in range(3)],
            pltpu.VMEM((tiles, pixels), jnp.int32),
            pltpu.VMEM((owners, 8, pixels), jnp.int32),
            pltpu.VMEM((owners, 8, pixels), jnp.int32),
            pltpu.VMEM(slot, BF16), pltpu.VMEM(slot, BF16),
            pltpu.VMEM(slot, F32), pltpu.VMEM(slot, F32),
            pltpu.VMEM(slot, BF16), pltpu.VMEM(slot, BF16),
            pltpu.VMEM(observed.shape, F32),
            pltpu.VMEM((planes, blocks * pixels, releases), BF16),
            *[pltpu.VMEM(rows, BF16) for _ in range(4)],
            pltpu.VMEM(rows[1:], F32),
            pltpu.VMEM((share, releases, releases), F32),
            pltpu.VMEM((PANEL * share, releases), F32),
            dma((7,)), dma,
            *[dma((owners,)) for _ in range(8)],
            *[dma((planes,)) for _ in range(4)],
            dma((planes, 2)), dma((planes, 2)),
        ],
        compiler_params=pltpu.CompilerParams(
            collective_id=0, has_side_effects=True, vmem_limit_bytes=60 * 2**20
        ),
        name="newton_step",
    )(
        footprint, block_tile, log_release.T, prior_mean.T, prior_weight.T, observed,
        noise_weight, pixel_mask,
    )
    return (updated.T, residual)


def solution(mesh):
    in_specs = (
        P(("groups", "rel", "bin", "rep"), None, None),
        P(("groups", "rel", "bin", "rep")),
        P(("groups", "rel"), None),
        P(("groups", "rel"), None),
        P(("groups", "rel"), None),
        P(("groups", "rel", "bin", "rep"), None, None),
        P(("groups", "rel", "bin", "rep"), None, None),
        P(("groups", "rel", "bin", "rep"), None),
    )
    out_specs = (
        P(("groups", "rel"), ("bin", "rep")),
        P(("groups", "rel", "bin", "rep"), None, None),
    )
    return jax.shard_map(body, mesh=mesh, in_specs=in_specs, out_specs=out_specs, check_vma=False)
```

```python
import functools
import math

import jax
import jax.numpy as jnp
from jax import lax
from jax.experimental import pallas as pl
from jax.experimental.pallas import tpu as pltpu
from jax.sharding import PartitionSpec as P

MESH = pl.DeviceIdType.MESH
F32, BF16 = jnp.float32, jnp.bfloat16
NN = (((1,), (0,)), ((), ()))
TN = (((0,), (0,)), ((), ()))
PANEL = 32


def dot(a, b, dims=NN):
    return lax.dot_general(a, b, dims, preferred_element_type=F32)


def split(x):
    high = x.astype(BF16)
    rest = x - high.astype(F32)
    middle = rest.astype(BF16)
    return high, middle, (rest - middle.astype(F32)).astype(BF16)


def step_kernel(
    owners, xs, share, cap,
    fp_hbm, bt, lr_hbm, mean_hbm, pw_hbm, obs_hbm, noise_hbm, mask_hbm,
    resid_hbm, updated,
    fp, far, obs, noise, resid, lr, mean, pw, mask,
    idx_send, idx_recv, w_send, w_recv, em_send, em_recv, r_send, r_recv,
    weight, ft, w_out, w_in, r_out, r_in, wrows,
    mat, pan,
    in_s, out_s,
    idx_ss, idx_rs, w_ss, w_rs, em_ss, em_rs, r_ss, r_rs,
    wp_ss, wp_rs, rp_ss, rp_rs, fp_ss, fp_rs,
):
    blocks, releases, pixels = fp.shape
    planes = 2 * xs
    tiles, bins, _ = obs.shape
    half = blocks // 2
    pack = 16 // share
    me, mx, mc = lax.axis_index("rel"), lax.axis_index("bin"), lax.axis_index("rep")

    def rel_id(step):
        return {"rel": lax.rem(me + step, owners)}

    def plane_id(dx, dc):
        return {"bin": lax.rem(mx + dx, xs), "rep": lax.rem(mc + dc, 2)}

    others = [(dx, dc) for dx in range(xs) for dc in range(2) if (dx, dc) != (0, 0)]

    def remote(src, dst, ss, rs, target):
        return pltpu.make_async_remote_copy(
            src_ref=src, dst_ref=dst, send_sem=ss, recv_sem=rs, device_id=target,
            device_id_type=MESH,
        )

    loads = [
        pltpu.make_async_copy(src, dst, in_s.at[n])
        for n, (src, dst) in enumerate((
            (lr_hbm, lr), (fp_hbm, fp), (mask_hbm, mask), (noise_hbm, noise), (obs_hbm, obs),
            (mean_hbm, mean), (pw_hbm, pw),
        ))
    ]
    for copy in loads:
        copy.start()
    barrier = pltpu.get_barrier_semaphore()
    for step in range(1, owners):
        pl.semaphore_signal(barrier, inc=1, device_id=rel_id(step), device_id_type=MESH)
    for dx, dc in others:
        pl.semaphore_signal(barrier, inc=1, device_id=plane_id(dx, dc), device_id_type=MESH)

    sub = lax.broadcasted_iota(jnp.int32, (8, pixels), 0)
    slots = {}
    for step in range(owners):
        first_tile = lax.rem(me + step, owners) * tiles
        start, end = jnp.int32(0), jnp.int32(0)
        for k in range(blocks):
            start += (bt[k] < first_tile).astype(jnp.int32)
            end += (bt[k] < first_tile + tiles).astype(jnp.int32)
        table = jnp.full((8, pixels), -1, jnp.int32)
        for j in range(cap):
            source = jnp.minimum(start + j, blocks - 1)
            used = start + j < end
            tile = jnp.where(used, bt[source] - first_tile, -1)
            slots[step, j] = source, used
            table = jnp.where(sub == j, tile, table)
        if step:
            idx_send[step] = table
        else:
            idx_recv[0] = table

    pl.semaphore_wait(barrier, owners - 1 + len(others))
    idx_copies = [
        remote(idx_send.at[s], idx_recv.at[s], idx_ss.at[s], idx_rs.at[s], rel_id(s))
        for s in range(1, owners)
    ]
    for copy in idx_copies:
        copy.start()
    piece = [pl.ds(h * half, half) for h in range(2)]
    across, over = {}, {}
    for h in range(2):
        for dx in range(1, xs):
            across[dx, h] = remote(
                fp_hbm.at[piece[h]], far.at[2 * dx, piece[h]],
                fp_ss.at[2 * dx, h], fp_rs.at[2 * dx, h], plane_id(dx, 0),
            )
            across[dx, h].start()
        over[0, h] = remote(
            fp_hbm.at[piece[h]], far.at[1, piece[h]], fp_ss.at[1, h], fp_rs.at[1, h],
            plane_id(0, 1),
        )
        over[0, h].start()

    loads[0].wait()
    rates = jnp.log1p(jnp.exp(-jnp.abs(lr[...]))) + jnp.maximum(lr[...], 0.0)
    rates = rates.astype(BF16)
    loads[1].wait()
    em_copies = []
    for step in [*range(1, owners), 0]:
        target = em_send if step else em_recv
        for j in range(cap):
            source, used = slots[step, j]
            emission = dot(rates, fp[source])
            target[step, j] = jnp.where(used, emission, 0.0)
        if step:
            copy = remote(
                em_send.at[step], em_recv.at[step], em_ss.at[step], em_rs.at[step], rel_id(step)
            )
            copy.start()
            em_copies.append(copy)

    loads[2].wait()
    loads[3].wait()
    for t in range(tiles):
        weight[t] = mask[t : t + 1, :].astype(F32) * noise[t]

    def turn(slot):
        blocks_here = far.at[slot] if slot else fp
        for k in range(blocks):
            ft[slot, k * pixels : (k + 1) * pixels, :] = blocks_here[k].T

    turn(0)

    back_ids = [rel_id(owners - s) for s in range(owners)]

    def pick(step, j, array):
        row = idx_recv[step][j : j + 1, :]
        total = jnp.zeros(array.shape[1:], F32)
        for t in range(tiles):
            total = jnp.where(row == t, array[t], total)
        return total.astype(BF16)

    w_copies = []
    for step in [*range(1, owners), 0]:
        if step:
            idx_copies[step - 1].wait_recv()
        target = w_send if step else w_recv
        for j in range(cap):
            target[step, j] = pick(step, j, weight)
        if step:
            copy = remote(
                w_send.at[step], w_recv.at[step], w_ss.at[step], w_rs.at[step], back_ids[step]
            )
            copy.start()
            w_copies.append(copy)
    loads[4].wait()
    for copy in em_copies:
        copy.wait_recv()
    for t in range(tiles):
        total = jnp.zeros((bins, pixels), F32)
        for step in range(owners):
            for j in range(cap):
                row = idx_recv[step][j : j + 1, :]
                total += jnp.where(row == t, em_recv[step, j], 0.0)
        resid[t] = weight[t] * (obs[t] - total)
    resid_out = pltpu.make_async_copy(resid, resid_hbm, out_s)
    resid_out.start()
    r_copies = []
    for step in [*range(1, owners), 0]:
        target = r_send if step else r_recv
        for j in range(cap):
            target[step, j] = pick(step, j, resid)
        if step:
            copy = remote(
                r_send.at[step], r_recv.at[step], r_ss.at[step], r_rs.at[step], back_ids[step]
            )
            copy.start()
            r_copies.append(copy)

    places = []
    for k in range(blocks):
        owner = bt[k] // tiles
        rank = jnp.int32(0)
        for back in range(1, cap):
            if k - back >= 0:
                rank += (bt[k - back] // tiles == owner).astype(jnp.int32)
        places.append((lax.rem(owner - me + owners, owners), rank))

    def to_plane(array, out, arrived, ss, rs):
        for k in range(0, blocks, pack):
            rows = [array[place].astype(F32) for place in places[k : k + pack]]
            for q in range(planes):
                wanted = [row[q * share : (q + 1) * share] for row in rows]
                wanted = jnp.concatenate(wanted, axis=0).astype(BF16)
                out[q, k * share : (k + pack) * share, :] = wanted
        copies = []
        for dx, dc in others:
            target, slot = plane_id(dx, dc), 2 * dx + dc
            copy = remote(
                out.at[target["bin"] * 2 + target["rep"]], arrived.at[slot],
                ss.at[slot], rs.at[slot], target,
            )
            copy.start()
            copies.append(copy)
        return copies

    here = mx * 2 + mc
    for copy in w_copies:
        copy.wait_recv()
    wp_copies = to_plane(w_recv, w_out, w_in, wp_ss, wp_rs)

    group = math.gcd(blocks, 6)

    def gram(slot, fresh):
        blocks_here = far.at[slot] if slot else fp

        def add(start):
            def pair(i):
                rows = []
                for b in range(2):
                    parts = []
                    for n in range(group):
                        w = wrows[pl.ds((start + n) * share + 2 * i + b, 1), :]
                        parts.append(blocks_here[start + n] * w.astype(BF16))
                    rows.append(jnp.concatenate(parts, axis=1))
                turned = ft[slot, pl.ds(pl.multiple_of(start * pixels, 128), group * pixels), :]
                total = dot(jnp.concatenate(rows, axis=0), turned)
                for b in range(2):
                    part = total[b * releases : (b + 1) * releases]
                    mat[2 * i + b] = part if fresh else mat[2 * i + b] + part

            for i in range(share // 2):
                pair(i)

        if blocks == group:
            add(0)
        else:
            if fresh:
                mat[...] = jnp.zeros_like(mat)
            fresh = False
            lax.fori_loop(0, blocks // group, lambda g, c: (add(g * group), c)[1], 0)

    def pass_on(h):
        for dx in range(1, xs):
            across[dx, h].wait_recv()
            over[dx, h] = remote(
                far.at[2 * dx, piece[h]], far.at[2 * dx + 1, piece[h]],
                fp_ss.at[2 * dx + 1, h], fp_rs.at[2 * dx + 1, h], plane_id(0, 1),
            )
            over[dx, h].start()

    pass_on(0)
    wrows[...] = w_out[here].astype(F32)
    gram(0, True)
    pass_on(1)

    for copy in r_copies:
        copy.wait_recv()
    rp_copies = to_plane(r_recv, r_out, r_in, rp_ss, rp_rs)

    for n, (dx, dc) in enumerate(others):
        slot = 2 * dx + dc
        for h in range(2):
            if dc:
                over[dx, h].wait_recv()
        wp_copies[n].wait_recv()
        turn(slot)
        wrows[...] = w_in[slot].astype(F32)
        gram(slot, False)

    loads[5].wait()
    loads[6].wait()
    first = (mx * 2 + mc) * share
    mine = pl.ds(pl.multiple_of(first, share), share)
    lr_t, mean_t, pw_t = (ref[mine, :] for ref in (lr, mean, pw))
    inverse_slope = 1.0 + jnp.exp(-lr_t)
    extra = pw_t * inverse_slope * inverse_slope

    row_id = lax.broadcasted_iota(jnp.int32, (releases, releases), 0)
    col_id = lax.broadcasted_iota(jnp.int32, (releases, releases), 1)
    on = row_id == col_id
    for b in range(share):
        square = mat[b]
        square = 0.5 * (square + square.T)
        mat[b] = jnp.where(on, square + extra[b : b + 1], square)

    invert(share, mat, pan)

    def side(array):
        wide = array.astype(F32)
        parts = [wide[k * share : (k + 1) * share] for k in range(blocks)]
        return jnp.concatenate(parts, axis=1).astype(BF16)

    total = dot(side(r_out[here]), ft[0])
    for n, (dx, dc) in enumerate(others):
        rp_copies[n].wait_recv()
        total += dot(side(r_in[2 * dx + dc]), ft[2 * dx + dc])
    right = total - pw_t * (lr_t - mean_t) * inverse_slope
    wide = jnp.concatenate([*split(right), jnp.zeros_like(right, BF16)], axis=0)
    sub_share = lax.broadcasted_iota(jnp.int32, (share, releases), 0)
    change = jnp.zeros((share, releases), F32)
    for b in range(share):
        high, middle, low = (dot(wide, part) for part in split(mat[b]))
        solved = (
            high[:share] + high[share : 2 * share] + high[2 * share : 3 * share]
            + middle[:share] + middle[share : 2 * share] + low[:share]
        )
        change = jnp.where(sub_share == b, solved, change)
    updated[...] = lr_t + change * inverse_slope

    for copy in [
        *idx_copies, *em_copies, *w_copies, *r_copies, *wp_copies, *rp_copies,
        *across.values(), *over.values(),
    ]:
        copy.wait_send()
    resid_out.wait()


def invert(share, mat, pan):
    releases = mat.shape[1]
    lane = lax.broadcasted_iota(jnp.int32, (share, releases), 1)
    col_id = lax.broadcasted_iota(jnp.int32, (releases, releases), 1)
    panel_lane = lax.broadcasted_iota(jnp.int32, (PANEL, releases), 1)
    for base in range(0, releases, PANEL):
        for b in range(share):
            pan[pl.ds(b, PANEL, stride=share), :] = mat[b, base : base + PANEL, :]
        rows = pan[...].reshape(PANEL, share, releases)
        for k in range(0, PANEL, 2):
            c = base + k
            f0 = jnp.broadcast_to(rows[:, :, c : c + 1], rows.shape)
            f1 = jnp.broadcast_to(rows[:, :, c + 1 : c + 2], rows.shape)
            p, q, r, s = f0[k], f1[k], f0[k + 1], f1[k + 1]
            scale = 1.0 / (p * s - q * r)
            at0, at1 = lane == c, lane == c + 1
            u0 = jnp.where(at0, 1.0, jnp.where(at1, 0.0, rows[k]))
            u1 = jnp.where(at1, 1.0, jnp.where(at0, 0.0, rows[k + 1]))
            n0 = (s * u0 - q * u1) * scale
            n1 = (p * u1 - r * u0) * scale
            pivots = jnp.concatenate([n0[None], n1[None]], axis=0)
            gone = (at0 | at1)[None]

            def reduce(a, z):
                kept = jnp.where(gone, 0.0, rows[a:z])
                return kept - f0[a:z] * n0[None] - f1[a:z] * n1[None]

            pieces = [reduce(0, k)] if k else []
            pieces.append(pivots)
            if k + 2 < PANEL:
                pieces.append(reduce(k + 2, PANEL))
            rows = jnp.concatenate(pieces, axis=0)
        pan[...] = rows.reshape(PANEL * share, releases)
        inside = (col_id >= base) & (col_id < base + PANEL)
        for b in range(share):
            old = mat[b]
            side = old[base : base + PANEL]
            side = jnp.where(panel_lane < base, -side, side)
            new = pan[pl.ds(b, PANEL, stride=share), :]
            sh, sm, sl = split(side)
            nh, nm, nl = split(new)
            left = jnp.concatenate([sh, sh, sm, sh, sl, sm], axis=0)
            right = jnp.concatenate([nh, nm, nh, nl, nh, nm], axis=0)
            moved = jnp.where(inside, 0.0, old) - dot(left, right, TN)
            mat[b] = moved
            mat[b, base : base + PANEL, :] = new


def hand_out_kernel(pieces, updated, residual, updated_out, residual_out, sems):
    size = residual.shape[0] // pieces
    copies = [pltpu.make_async_copy(updated, updated_out, sems.at[pieces])]
    for n in range(pieces):
        part = pl.ds(n * size, size)
        copies.append(
            pltpu.make_async_copy(residual.at[part], residual_out.at[part], sems.at[n])
        )
    for copy in copies:
        copy.start()
    for copy in copies:
        copy.wait()


def body(
    footprint, block_tile, log_release, prior_mean, prior_weight, observed, noise_weight, pixel_mask
):
    blocks, releases, pixels = footprint.shape
    tiles, bins, _ = observed.shape
    owners, xs = lax.axis_size("rel"), lax.axis_size("bin")
    cap = blocks * 4 // 3 // owners
    planes = 2 * xs
    share = bins // planes
    vmem = pl.BlockSpec(memory_space=pltpu.VMEM)
    smem = pl.BlockSpec(memory_space=pltpu.SMEM)
    dma = pltpu.SemaphoreType.DMA
    slot = (owners, cap, bins, pixels)
    rows = (planes, blocks * share, pixels)
    hbm = pl.BlockSpec(memory_space=pltpu.HBM)
    residual, updated = pl.pallas_call(
        functools.partial(step_kernel, owners, xs, share, cap),
        out_shape=(
            jax.ShapeDtypeStruct(observed.shape, F32),
            jax.ShapeDtypeStruct((share, releases), F32),
        ),
        in_specs=[hbm, smem, hbm, hbm, hbm, hbm, hbm, hbm],
        out_specs=(hbm, vmem),
        scratch_shapes=[
            pltpu.VMEM(footprint.shape, BF16),
            pltpu.VMEM((planes, *footprint.shape), BF16),
            *[pltpu.VMEM(observed.shape, F32) for _ in range(3)],
            *[pltpu.VMEM((bins, releases), F32) for _ in range(3)],
            pltpu.VMEM((tiles, pixels), jnp.int32),
            pltpu.VMEM((owners, 8, pixels), jnp.int32),
            pltpu.VMEM((owners, 8, pixels), jnp.int32),
            pltpu.VMEM(slot, BF16), pltpu.VMEM(slot, BF16),
            pltpu.VMEM(slot, F32), pltpu.VMEM(slot, F32),
            pltpu.VMEM(slot, BF16), pltpu.VMEM(slot, BF16),
            pltpu.VMEM(observed.shape, F32),
            pltpu.VMEM((planes, blocks * pixels, releases), BF16),
            *[pltpu.VMEM(rows, BF16) for _ in range(4)],
            pltpu.VMEM(rows[1:], F32),
            pltpu.VMEM((share, releases, releases), F32),
            pltpu.VMEM((PANEL * share, releases), F32),
            dma((7,)), dma,
            *[dma((owners,)) for _ in range(8)],
            *[dma((planes,)) for _ in range(4)],
            dma((planes, 2)), dma((planes, 2)),
        ],
        compiler_params=pltpu.CompilerParams(
            collective_id=0, has_side_effects=True, vmem_limit_bytes=60 * 2**20
        ),
        name="newton_step",
    )(
        footprint, block_tile, log_release.T, prior_mean.T, prior_weight.T, observed,
        noise_weight, pixel_mask,
    )
    pieces = math.gcd(tiles, 4)
    updated, residual = pl.pallas_call(
        functools.partial(hand_out_kernel, pieces),
        out_shape=(
            jax.ShapeDtypeStruct(updated.shape, F32),
            jax.ShapeDtypeStruct(residual.shape, F32),
        ),
        in_specs=[hbm, hbm],
        out_specs=(hbm, hbm),
        scratch_shapes=[dma((pieces + 1,))],
        compiler_params=pltpu.CompilerParams(vmem_limit_bytes=60 * 2**20),
        name="hand_out",
    )(updated, residual)
    return (updated.T, residual)


def solution(mesh):
    in_specs = (
        P(("groups", "rel", "bin", "rep"), None, None),
        P(("groups", "rel", "bin", "rep")),
        P(("groups", "rel"), None),
        P(("groups", "rel"), None),
        P(("groups", "rel"), None),
        P(("groups", "rel", "bin", "rep"), None, None),
        P(("groups", "rel", "bin", "rep"), None, None),
        P(("groups", "rel", "bin", "rep"), None),
    )
    out_specs = (
        P(("groups", "rel"), ("bin", "rep")),
        P(("groups", "rel", "bin", "rep"), None, None),
    )
    return jax.shard_map(body, mesh=mesh, in_specs=in_specs, out_specs=out_specs, check_vma=False)
```

```python
import functools
import math

import jax
import jax.numpy as jnp
from jax import lax
from jax.experimental import pallas as pl
from jax.experimental.pallas import tpu as pltpu
from jax.sharding import PartitionSpec as P

MESH = pl.DeviceIdType.MESH
F32, BF16 = jnp.float32, jnp.bfloat16
NN = (((1,), (0,)), ((), ()))
TN = (((0,), (0,)), ((), ()))
PANEL = 32


def dot(a, b, dims=NN):
    return lax.dot_general(a, b, dims, preferred_element_type=F32)


def split(x):
    high = x.astype(BF16)
    rest = x - high.astype(F32)
    middle = rest.astype(BF16)
    return high, middle, (rest - middle.astype(F32)).astype(BF16)


def step_kernel(
    owners, xs, share, cap,
    fp_hbm, bt, lr_hbm, mean_hbm, pw_hbm, obs_hbm, noise_hbm, mask_hbm,
    resid_hbm, updated,
    fp, far, obs, noise, resid, lr, mean, pw, mask,
    idx_send, idx_recv, w_send, w_recv, em_send, em_recv, r_send, r_recv,
    weight, ft, w_out, w_in, r_out, r_in, wrows,
    mat, pan,
    in_s, out_s,
    idx_ss, idx_rs, w_ss, w_rs, em_ss, em_rs, r_ss, r_rs,
    wp_ss, wp_rs, rp_ss, rp_rs, fp_ss, fp_rs,
):
    blocks, releases, pixels = fp.shape
    planes = 2 * xs
    tiles, bins, _ = obs.shape
    half = blocks // 2
    pack = 16 // share
    me, mx, mc = lax.axis_index("rel"), lax.axis_index("bin"), lax.axis_index("rep")

    def rel_id(step):
        return {"rel": lax.rem(me + step, owners)}

    def plane_id(dx, dc):
        return {"bin": lax.rem(mx + dx, xs), "rep": lax.rem(mc + dc, 2)}

    others = [(dx, dc) for dx in range(xs) for dc in range(2) if (dx, dc) != (0, 0)]

    def remote(src, dst, ss, rs, target):
        return pltpu.make_async_remote_copy(
            src_ref=src, dst_ref=dst, send_sem=ss, recv_sem=rs, device_id=target,
            device_id_type=MESH,
        )

    loads = [
        pltpu.make_async_copy(src, dst, in_s.at[n])
        for n, (src, dst) in enumerate((
            (lr_hbm, lr), (fp_hbm, fp), (mask_hbm, mask), (noise_hbm, noise), (obs_hbm, obs),
            (mean_hbm, mean), (pw_hbm, pw),
        ))
    ]
    for copy in loads:
        copy.start()
    barrier = pltpu.get_barrier_semaphore()
    for step in range(1, owners):
        pl.semaphore_signal(barrier, inc=1, device_id=rel_id(step), device_id_type=MESH)
    for dx, dc in others:
        pl.semaphore_signal(barrier, inc=1, device_id=plane_id(dx, dc), device_id_type=MESH)

    sub = lax.broadcasted_iota(jnp.int32, (8, pixels), 0)
    slots = {}
    for step in range(owners):
        first_tile = lax.rem(me + step, owners) * tiles
        start, end = jnp.int32(0), jnp.int32(0)
        for k in range(blocks):
            start += (bt[k] < first_tile).astype(jnp.int32)
            end += (bt[k] < first_tile + tiles).astype(jnp.int32)
        table = jnp.full((8, pixels), -1, jnp.int32)
        for j in range(cap):
            source = jnp.minimum(start + j, blocks - 1)
            used = start + j < end
            tile = jnp.where(used, bt[source] - first_tile, -1)
            slots[step, j] = source, used
            table = jnp.where(sub == j, tile, table)
        if step:
            idx_send[step] = table
        else:
            idx_recv[0] = table

    pl.semaphore_wait(barrier, owners - 1 + len(others))
    idx_copies = [
        remote(idx_send.at[s], idx_recv.at[s], idx_ss.at[s], idx_rs.at[s], rel_id(s))
        for s in range(1, owners)
    ]
    for copy in idx_copies:
        copy.start()
    piece = [pl.ds(h * half, half) for h in range(2)]
    across, over = {}, {}
    for h in range(2):
        for dx in range(1, xs):
            across[dx, h] = remote(
                fp_hbm.at[piece[h]], far.at[2 * dx, piece[h]],
                fp_ss.at[2 * dx, h], fp_rs.at[2 * dx, h], plane_id(dx, 0),
            )
            across[dx, h].start()
        over[0, h] = remote(
            fp_hbm.at[piece[h]], far.at[1, piece[h]], fp_ss.at[1, h], fp_rs.at[1, h],
            plane_id(0, 1),
        )
        over[0, h].start()

    loads[0].wait()
    rates = jnp.log1p(jnp.exp(-jnp.abs(lr[...]))) + jnp.maximum(lr[...], 0.0)
    rates = rates.astype(BF16)
    loads[1].wait()
    em_copies = []
    for step in [*range(1, owners), 0]:
        target = em_send if step else em_recv
        for j in range(cap):
            source, used = slots[step, j]
            emission = dot(rates, fp[source])
            target[step, j] = jnp.where(used, emission, 0.0)
        if step:
            copy = remote(
                em_send.at[step], em_recv.at[step], em_ss.at[step], em_rs.at[step], rel_id(step)
            )
            copy.start()
            em_copies.append(copy)

    loads[2].wait()
    loads[3].wait()
    for t in range(tiles):
        weight[t] = mask[t : t + 1, :].astype(F32) * noise[t]

    def turn(slot):
        blocks_here = far.at[slot] if slot else fp
        for k in range(blocks):
            ft[slot, k * pixels : (k + 1) * pixels, :] = blocks_here[k].T

    turn(0)

    back_ids = [rel_id(owners - s) for s in range(owners)]

    def pick(step, j, array):
        row = idx_recv[step][j : j + 1, :]
        total = jnp.zeros(array.shape[1:], F32)
        for t in range(tiles):
            total = jnp.where(row == t, array[t], total)
        return total.astype(BF16)

    w_copies = []
    for step in [*range(1, owners), 0]:
        if step:
            idx_copies[step - 1].wait_recv()
        target = w_send if step else w_recv
        for j in range(cap):
            target[step, j] = pick(step, j, weight)
        if step:
            copy = remote(
                w_send.at[step], w_recv.at[step], w_ss.at[step], w_rs.at[step], back_ids[step]
            )
            copy.start()
            w_copies.append(copy)
    loads[4].wait()
    for copy in em_copies:
        copy.wait_recv()
    for t in range(tiles):
        total = jnp.zeros((bins, pixels), F32)
        for step in range(owners):
            for j in range(cap):
                row = idx_recv[step][j : j + 1, :]
                total += jnp.where(row == t, em_recv[step, j], 0.0)
        resid[t] = weight[t] * (obs[t] - total)
    resid_out = pltpu.make_async_copy(resid, resid_hbm, out_s)
    resid_out.start()
    r_copies = []
    for step in [*range(1, owners), 0]:
        target = r_send if step else r_recv
        for j in range(cap):
            target[step, j] = pick(step, j, resid)
        if step:
            copy = remote(
                r_send.at[step], r_recv.at[step], r_ss.at[step], r_rs.at[step], back_ids[step]
            )
            copy.start()
            r_copies.append(copy)

    places = []
    for k in range(blocks):
        owner = bt[k] // tiles
        rank = jnp.int32(0)
        for back in range(1, cap):
            if k - back >= 0:
                rank += (bt[k - back] // tiles == owner).astype(jnp.int32)
        places.append((lax.rem(owner - me + owners, owners), rank))

    def to_plane(array, out, arrived, ss, rs):
        for k in range(0, blocks, pack):
            rows = [array[place].astype(F32) for place in places[k : k + pack]]
            for q in range(planes):
                wanted = [row[q * share : (q + 1) * share] for row in rows]
                wanted = jnp.concatenate(wanted, axis=0).astype(BF16)
                out[q, k * share : (k + pack) * share, :] = wanted
        copies = []
        for dx, dc in others:
            target, slot = plane_id(dx, dc), 2 * dx + dc
            copy = remote(
                out.at[target["bin"] * 2 + target["rep"]], arrived.at[slot],
                ss.at[slot], rs.at[slot], target,
            )
            copy.start()
            copies.append(copy)
        return copies

    here = mx * 2 + mc
    for copy in w_copies:
        copy.wait_recv()
    wp_copies = to_plane(w_recv, w_out, w_in, wp_ss, wp_rs)

    group = math.gcd(blocks, 6)

    def gram(slot, fresh):
        blocks_here = far.at[slot] if slot else fp

        def add(start):
            def pair(i):
                rows = []
                for b in range(2):
                    parts = []
                    for n in range(group):
                        w = wrows[pl.ds((start + n) * share + 2 * i + b, 1), :]
                        parts.append(blocks_here[start + n] * w.astype(BF16))
                    rows.append(jnp.concatenate(parts, axis=1))
                turned = ft[slot, pl.ds(pl.multiple_of(start * pixels, 128), group * pixels), :]
                total = dot(jnp.concatenate(rows, axis=0), turned)
                for b in range(2):
                    part = total[b * releases : (b + 1) * releases]
                    mat[2 * i + b] = part if fresh else mat[2 * i + b] + part

            for i in range(share // 2):
                pair(i)

        if blocks == group:
            add(0)
        else:
            if fresh:
                mat[...] = jnp.zeros_like(mat)
            fresh = False
            lax.fori_loop(0, blocks // group, lambda g, c: (add(g * group), c)[1], 0)

    def pass_on(h):
        for dx in range(1, xs):
            across[dx, h].wait_recv()
            over[dx, h] = remote(
                far.at[2 * dx, piece[h]], far.at[2 * dx + 1, piece[h]],
                fp_ss.at[2 * dx + 1, h], fp_rs.at[2 * dx + 1, h], plane_id(0, 1),
            )
            over[dx, h].start()

    pass_on(0)
    wrows[...] = w_out[here].astype(F32)
    gram(0, True)
    pass_on(1)

    for copy in r_copies:
        copy.wait_recv()
    rp_copies = to_plane(r_recv, r_out, r_in, rp_ss, rp_rs)

    for n, (dx, dc) in enumerate(others):
        slot = 2 * dx + dc
        for h in range(2):
            if dc:
                over[dx, h].wait_recv()
        wp_copies[n].wait_recv()
        turn(slot)
        wrows[...] = w_in[slot].astype(F32)
        gram(slot, False)

    loads[5].wait()
    loads[6].wait()
    first = (mx * 2 + mc) * share
    mine = pl.ds(pl.multiple_of(first, share), share)
    lr_t, mean_t, pw_t = (ref[mine, :] for ref in (lr, mean, pw))
    inverse_slope = 1.0 + jnp.exp(-lr_t)
    extra = pw_t * inverse_slope * inverse_slope

    row_id = lax.broadcasted_iota(jnp.int32, (releases, releases), 0)
    col_id = lax.broadcasted_iota(jnp.int32, (releases, releases), 1)
    on = row_id == col_id
    for b in range(share):
        square = mat[b]
        square = 0.5 * (square + square.T)
        mat[b] = jnp.where(on, square + extra[b : b + 1], square)

    invert(share, mat, pan)

    def side(array):
        wide = array.astype(F32)
        parts = [wide[k * share : (k + 1) * share] for k in range(blocks)]
        return jnp.concatenate(parts, axis=1).astype(BF16)

    total = dot(side(r_out[here]), ft[0])
    for n, (dx, dc) in enumerate(others):
        rp_copies[n].wait_recv()
        total += dot(side(r_in[2 * dx + dc]), ft[2 * dx + dc])
    right = total - pw_t * (lr_t - mean_t) * inverse_slope
    wide = jnp.concatenate([*split(right), jnp.zeros_like(right, BF16)], axis=0)
    sub_share = lax.broadcasted_iota(jnp.int32, (share, releases), 0)
    change = jnp.zeros((share, releases), F32)
    for b in range(share):
        high, middle, low = (dot(wide, part) for part in split(mat[b]))
        solved = (
            high[:share] + high[share : 2 * share] + high[2 * share : 3 * share]
            + middle[:share] + middle[share : 2 * share] + low[:share]
        )
        change = jnp.where(sub_share == b, solved, change)
    updated[...] = lr_t + change * inverse_slope

    for copy in [
        *idx_copies, *em_copies, *w_copies, *r_copies, *wp_copies, *rp_copies,
        *across.values(), *over.values(),
    ]:
        copy.wait_send()
    resid_out.wait()


def invert(share, mat, pan):
    releases = mat.shape[1]
    lane = lax.broadcasted_iota(jnp.int32, (share, releases), 1)
    col_id = lax.broadcasted_iota(jnp.int32, (releases, releases), 1)
    panel_lane = lax.broadcasted_iota(jnp.int32, (PANEL, releases), 1)
    for base in range(0, releases, PANEL):
        for b in range(share):
            pan[pl.ds(b, PANEL, stride=share), :] = mat[b, base : base + PANEL, :]
        rows = pan[...].reshape(PANEL, share, releases)
        for k in range(0, PANEL, 2):
            c = base + k
            f0 = jnp.broadcast_to(rows[:, :, c : c + 1], rows.shape)
            f1 = jnp.broadcast_to(rows[:, :, c + 1 : c + 2], rows.shape)
            p, q, r, s = f0[k], f1[k], f0[k + 1], f1[k + 1]
            scale = 1.0 / (p * s - q * r)
            at0, at1 = lane == c, lane == c + 1
            u0 = jnp.where(at0, 1.0, jnp.where(at1, 0.0, rows[k]))
            u1 = jnp.where(at1, 1.0, jnp.where(at0, 0.0, rows[k + 1]))
            n0 = (s * u0 - q * u1) * scale
            n1 = (p * u1 - r * u0) * scale
            pivots = jnp.concatenate([n0[None], n1[None]], axis=0)
            gone = (at0 | at1)[None]

            def reduce(a, z):
                kept = jnp.where(gone, 0.0, rows[a:z])
                return kept - f0[a:z] * n0[None] - f1[a:z] * n1[None]

            pieces = [reduce(0, k)] if k else []
            pieces.append(pivots)
            if k + 2 < PANEL:
                pieces.append(reduce(k + 2, PANEL))
            rows = jnp.concatenate(pieces, axis=0)
        pan[...] = rows.reshape(PANEL * share, releases)
        inside = (col_id >= base) & (col_id < base + PANEL)
        for b in range(share):
            old = mat[b]
            side = old[base : base + PANEL]
            side = jnp.where(panel_lane < base, -side, side)
            new = pan[pl.ds(b, PANEL, stride=share), :]
            sh, sm, sl = split(side)
            nh, nm, nl = split(new)
            left = jnp.concatenate([sh, sh, sm, sh, sl, sm], axis=0)
            right = jnp.concatenate([nh, nm, nh, nl, nh, nm], axis=0)
            moved = jnp.where(inside, 0.0, old) - dot(left, right, TN)
            mat[b] = moved
            mat[b, base : base + PANEL, :] = new


def hand_out_kernel(
    pieces, updated, residual, updated_out, residual_out, small, large, in_s, out_s
):
    size = residual.shape[0] // pieces
    parts = [pl.ds(n * size, size) for n in range(pieces)]
    views = [(updated, small, updated_out)]
    views += [(residual.at[p], large.at[p], residual_out.at[p]) for p in parts]
    arriving = [
        pltpu.make_async_copy(src, mid, in_s.at[n]) for n, (src, mid, _) in enumerate(views)
    ]
    leaving = [
        pltpu.make_async_copy(mid, dst, out_s.at[n]) for n, (_, mid, dst) in enumerate(views)
    ]
    for copy in arriving:
        copy.start()
    for first, second in zip(arriving, leaving):
        first.wait()
        second.start()
    for copy in leaving:
        copy.wait()


def body(
    footprint, block_tile, log_release, prior_mean, prior_weight, observed, noise_weight, pixel_mask
):
    blocks, releases, pixels = footprint.shape
    tiles, bins, _ = observed.shape
    owners, xs = lax.axis_size("rel"), lax.axis_size("bin")
    cap = blocks * 4 // 3 // owners
    planes = 2 * xs
    share = bins // planes
    vmem = pl.BlockSpec(memory_space=pltpu.VMEM)
    smem = pl.BlockSpec(memory_space=pltpu.SMEM)
    dma = pltpu.SemaphoreType.DMA
    slot = (owners, cap, bins, pixels)
    rows = (planes, blocks * share, pixels)
    hbm = pl.BlockSpec(memory_space=pltpu.HBM)
    residual, updated = pl.pallas_call(
        functools.partial(step_kernel, owners, xs, share, cap),
        out_shape=(
            jax.ShapeDtypeStruct(observed.shape, F32),
            jax.ShapeDtypeStruct((share, releases), F32),
        ),
        in_specs=[hbm, smem, hbm, hbm, hbm, hbm, hbm, hbm],
        out_specs=(hbm, vmem),
        scratch_shapes=[
            pltpu.VMEM(footprint.shape, BF16),
            pltpu.VMEM((planes, *footprint.shape), BF16),
            *[pltpu.VMEM(observed.shape, F32) for _ in range(3)],
            *[pltpu.VMEM((bins, releases), F32) for _ in range(3)],
            pltpu.VMEM((tiles, pixels), jnp.int32),
            pltpu.VMEM((owners, 8, pixels), jnp.int32),
            pltpu.VMEM((owners, 8, pixels), jnp.int32),
            pltpu.VMEM(slot, BF16), pltpu.VMEM(slot, BF16),
            pltpu.VMEM(slot, F32), pltpu.VMEM(slot, F32),
            pltpu.VMEM(slot, BF16), pltpu.VMEM(slot, BF16),
            pltpu.VMEM(observed.shape, F32),
            pltpu.VMEM((planes, blocks * pixels, releases), BF16),
            *[pltpu.VMEM(rows, BF16) for _ in range(4)],
            pltpu.VMEM(rows[1:], F32),
            pltpu.VMEM((share, releases, releases), F32),
            pltpu.VMEM((PANEL * share, releases), F32),
            dma((7,)), dma,
            *[dma((owners,)) for _ in range(8)],
            *[dma((planes,)) for _ in range(4)],
            dma((planes, 2)), dma((planes, 2)),
        ],
        compiler_params=pltpu.CompilerParams(
            collective_id=0, has_side_effects=True, vmem_limit_bytes=60 * 2**20
        ),
        name="newton_step",
    )(
        footprint, block_tile, log_release.T, prior_mean.T, prior_weight.T, observed,
        noise_weight, pixel_mask,
    )
    pieces = math.gcd(tiles, 2)
    updated, residual = pl.pallas_call(
        functools.partial(hand_out_kernel, pieces),
        out_shape=(
            jax.ShapeDtypeStruct(updated.shape, F32),
            jax.ShapeDtypeStruct(residual.shape, F32),
        ),
        in_specs=[hbm, hbm],
        out_specs=(hbm, hbm),
        scratch_shapes=[
            pltpu.VMEM(updated.shape, F32), pltpu.VMEM(residual.shape, F32),
            dma((pieces + 1,)), dma((pieces + 1,)),
        ],
        compiler_params=pltpu.CompilerParams(vmem_limit_bytes=60 * 2**20),
        name="hand_out",
    )(updated, residual)
    return (updated.T, residual)


def solution(mesh):
    in_specs = (
        P(("groups", "rel", "bin", "rep"), None, None),
        P(("groups", "rel", "bin", "rep")),
        P(("groups", "rel"), None),
        P(("groups", "rel"), None),
        P(("groups", "rel"), None),
        P(("groups", "rel", "bin", "rep"), None, None),
        P(("groups", "rel", "bin", "rep"), None, None),
        P(("groups", "rel", "bin", "rep"), None),
    )
    out_specs = (
        P(("groups", "rel"), ("bin", "rep")),
        P(("groups", "rel", "bin", "rep"), None, None),
    )
    return jax.shard_map(body, mesh=mesh, in_specs=in_specs, out_specs=out_specs, check_vma=False)
```
